32 devices in a mesh: dp: 8 (over z, x), segment: 2 (over core), mp: 2 (over y).
Axes of the slice: x: 2, y: 2, z: 4, core: 2. Of those that a mesh axis runs over, the one named last changes fastest.
Arguments:
- frames: bfloat16 [2, 2048, 1280], P(None, ('dp', 'mp')), may hold values from -8 to 8
- dec_states: bfloat16 [2, 512, 1280], P(None, 'dp'), may hold values from -8 to 8
- out_grad: bfloat16 [2, 512, 1280], P(None, 'dp'), may hold values from -3 to 3
- frame_lengths: int32 [2, 8, 4], P(None, 'dp'), may hold values from 1 to 128, 256 in all within a row
- token_lengths: int32 [2, 8, 4], P(None, 'dp'), may hold values from 1 to 32, 64 in all within a row
- weights: bfloat16 [2, 4, 1024, 1280], P('segment', None, 'mp'), may hold values from -1 to 1
- norm_gains: float32 [3, 1280], replicated, may hold values from 0.25 to 1.75
- norm_biases: float32 [3, 1280], replicated, may hold values from -2 to 2
Outputs:
- gradient: float32 [2, 3, 1024, 1280], P('segment', None, 'mp')
The draws below stay inside these ranges and needn't reach their ends.
Inputs may be any that keep to these rules, and one draw needn't show every extreme that they name: `frame_lengths`: the 4 utterance lengths of each micro-batch and group sum to 256. `token_lengths`: the 4 token counts of each micro-batch and group sum to 64.
All inputs are finite; a program needn't handle non-finite values.
Results may differ from the reference program's by a relative error of at most 0.04.
Values may be sent and summed in bfloat16 or wider, within the bound.
A program may use at most 64 MiB of HBM per device.

```python
import math
import jax
import jax.numpy as jnp
import numpy as np
from jax import lax

D = 1280
HS = 64
FRM = 256
TKM = 64
UTT = 4
MB = 2
HD = 1024
GROUPS = 8
FRAMES = 2048
TOKENS = 512
N_DP = 8
N_MP = 2


def drawn_rows(key, salt, shape):
    drawn_values = jax.random.truncated_normal(jax.random.fold_in(key, salt), -6.0, 6.0, shape, jnp.float32)
    return drawn_values


def draw_frames(key, part):
    return drawn_rows(key, 11, (MB, FRAMES, D)).astype(jnp.bfloat16)


def draw_dec_states(key, part):
    return drawn_rows(key, 21, (MB, TOKENS, D)).astype(jnp.bfloat16)


def draw_weights(key, part):
    drawn_values = jax.random.truncated_normal(jax.random.fold_in(key, 31), -6.0, 6.0, (2, 4, HD, D), jnp.float32) / math.sqrt(D)
    return drawn_values.astype(jnp.bfloat16)


def steps_of(rng, dims, pieces, smallest, largest):
    def one(dim, shards_of):
        steps = jax.random.uniform(jax.random.fold_in(jax.random.fold_in(rng, 6), dim), (shards_of,), jnp.float32, smallest / len(pieces), largest / len(pieces))
        return jnp.repeat(jnp.exp(steps), dims[dim] // shards_of).reshape((-1,) + (1,) * (len(dims) - dim - 1))

    factor_of = one(*pieces[0])
    for cut in pieces[1:]:
        factor_of = factor_of * one(*cut)
    return factor_of


def profile(amount, total, most, lean):
    weights = [(1 << 20) // math.isqrt(rank ** lean) + 1 for rank in range(2, amount + 1)]
    rest, counts = total - most - (amount - 1), [1] * (amount - 1)
    while rest > 0:
        free = [i for i in range(amount - 1) if counts[i] < most]
        whole, left = sum([weights[i] for i in free]), rest
        for i in free:
            more = min(most - counts[i], max(1, left * weights[i] // whole), rest)
            counts[i] = counts[i] + more
            rest = rest - more
    return np.array([most] + counts)


def uneven_parts(own_key, amount, total, reach, slope):
    if amount == 2:
        one = jax.random.randint(own_key, (), max(1, total - reach), min(reach, total - 1) + 1)
        return jnp.stack([one, total - one])
    sizes = jnp.asarray(profile(amount, total, reach, slope), jnp.int32)
    pairs = (amount - 1) // 2
    source_of, sink = sizes[1:1 + 2 * pairs:2], sizes[2:2 + 2 * pairs:2]
    slack = jnp.minimum(source_of - 1, reach - sink)
    moved = jax.random.randint(jax.random.fold_in(own_key, 1), (pairs,), 0, 1 << 20) % (slack + 1)
    sizes = sizes.at[1:1 + 2 * pairs:2].set(source_of - moved).at[2:2 + 2 * pairs:2].set(sink + moved)
    return sizes[jax.random.permutation(jax.random.fold_in(own_key, 2), amount)]


def scatter_about(stream_key, extent, deviation, reach, shards=(), kind=jnp.bfloat16):
    result = deviation * jax.random.normal(stream_key, extent, jnp.float32)
    if shards:
        result = result * steps_of(stream_key, extent, shards, -0.22, 0.18)
    return jnp.clip(result, -reach, reach).astype(kind)


def setup_inputs(seed: int = 0) -> dict:
    key_of = jax.random.split(jax.random.key(seed), 9)
    return {
        "frames": draw_frames(jax.random.fold_in(key_of[8], 71), 0),
        "dec_states": draw_dec_states(jax.random.fold_in(key_of[8], 71), 0),
        "out_grad": scatter_about(key_of[2], (MB, TOKENS, D), 0.5, 3.0, ((1, 8),)),
        "frame_lengths": jax.vmap(lambda own: uneven_parts(own, UTT, FRM, FRM // 2, 2))(jax.random.split(key_of[3], MB * GROUPS)).reshape((MB, GROUPS, UTT)).astype(jnp.int32),
        "token_lengths": jax.vmap(lambda own: uneven_parts(own, UTT, TKM, TKM // 2, 2))(jax.random.split(key_of[4], MB * GROUPS)).reshape((MB, GROUPS, UTT)).astype(jnp.int32),
        "weights": draw_weights(jax.random.fold_in(key_of[8], 71), 0),
        "norm_gains": jnp.clip(1.0 + 0.15 * jax.random.normal(key_of[6], (3, D), jnp.float32), 0.25, 1.75),
        "norm_biases": scatter_about(key_of[7], (3, D), 0.3, 2.0, (), jnp.float32),
    }


EPSILON = 1e-05

def layer_norm(values, norm_gain, offset):
    center = values - lax.optimization_barrier(jnp.mean(values, axis=-1, keepdims=True))
    variance = lax.optimization_barrier(jnp.mean(center * center, axis=-1, keepdims=True))
    return center * lax.rsqrt(variance + EPSILON) * norm_gain + offset

def norm_backward(grad_out, values, norm_gain):
    center = values - lax.optimization_barrier(jnp.mean(values, axis=-1, keepdims=True))
    variance = lax.optimization_barrier(jnp.mean(center * center, axis=-1, keepdims=True))
    inverse = lax.rsqrt(variance + EPSILON)
    normed = center * inverse
    scaled = grad_out * norm_gain
    return inverse * (scaled - lax.optimization_barrier(jnp.mean(scaled, axis=-1, keepdims=True)) - normed * lax.optimization_barrier(jnp.mean(scaled * normed, axis=-1, keepdims=True)))

def utterance_ids(lengths, row_count):
    bounds = jnp.cumsum(lengths, dtype=jnp.int32)
    places = jnp.arange(row_count, dtype=jnp.int32)
    return lax.optimization_barrier(jnp.sum((places[:, None] >= bounds[None, :]).astype(jnp.int32), axis=1))

def project(row_block, matrix):
    return jnp.dot(row_block, matrix.T, preferred_element_type=jnp.float32).astype(jnp.bfloat16)

def outer_rows(left_rows, right_rows):
    return jnp.dot(left_rows.T, right_rows, preferred_element_type=jnp.float32)

def split_heads(row_block):
    return row_block.astype(jnp.float32).reshape(row_block.shape[0], -1, HS)

def rounded_copy(values):
    return lax.optimization_barrier(values.astype(jnp.bfloat16)).astype(jnp.float32)

def attend(queries, key_rows, value_rows, allowed):
    scaling = 1.0 / math.sqrt(HS)
    scores = jnp.einsum('qhd,khd->hqk', split_heads(queries), split_heads(key_rows)) * scaling
    scores = jnp.where(allowed[None], scores, -1e+30)
    highest = lax.optimization_barrier(jnp.max(scores, axis=-1, keepdims=True))
    raised = jnp.exp(scores - highest)
    attn_probs = raised / lax.optimization_barrier(jnp.sum(raised, axis=-1, keepdims=True))
    context = jnp.einsum('hqk,khd->qhd', rounded_copy(attn_probs), split_heads(value_rows))
    return (context.reshape(queries.shape[0], -1).astype(jnp.bfloat16), attn_probs)

def attend_backward(queries, key_rows, value_rows, attn_probs, grad_context):
    scaling = 1.0 / math.sqrt(HS)
    grad_heads = split_heads(grad_context)
    grad_probs = jnp.einsum('qhd,khd->hqk', grad_heads, split_heads(value_rows))
    grad_scores = attn_probs * (grad_probs - lax.optimization_barrier(jnp.sum(grad_probs * attn_probs, axis=-1, keepdims=True)))
    grad_scores = rounded_copy(grad_scores)
    key_grad = jnp.einsum('hqk,qhd->khd', grad_scores, split_heads(queries)) * scaling
    key_grad = key_grad.reshape(key_rows.shape[0], -1).astype(jnp.bfloat16)
    value_grad = jnp.einsum('hqk,qhd->khd', rounded_copy(attn_probs), grad_heads)
    value_grad = value_grad.reshape(key_rows.shape[0], -1).astype(jnp.bfloat16)
    return (key_grad, value_grad)

def blocked_sum(products):
    gathered = None
    for left_rows, right_rows in products:
        left_split = left_rows.astype(jnp.float32).reshape(left_rows.shape[0], N_MP, -1)
        right_split = right_rows.astype(jnp.float32).reshape(N_MP, -1, right_rows.shape[1])
        piece_sum = jnp.einsum('rjc,jcd->jrd', left_split, right_split)
        gathered = piece_sum if gathered is None else gathered + piece_sum
    return lax.optimization_barrier(jnp.sum(rounded_copy(gathered), axis=0))

def group_terms(frames_group, tokens_group, upstream_group, frame_lens, token_lens, weights, norm_gains, norm_biases):
    encoder_sum = jnp.zeros((3, HD, D), jnp.float32)
    decoder_sum = jnp.zeros((3, HD, D), jnp.float32)
    for micro_index in range(MB):
        frame_ids = utterance_ids(frame_lens[micro_index], FRM)
        token_ids = utterance_ids(token_lens[micro_index], TKM)
        inputs = frames_group[micro_index]
        normed = layer_norm(inputs.astype(jnp.float32), norm_gains[0], norm_biases[0]).astype(jnp.bfloat16)
        queries = project(normed, weights[0, 0])
        key_rows = project(normed, weights[0, 1])
        value_rows = project(normed, weights[0, 2])
        context, attn_probs = attend(queries, key_rows, value_rows, frame_ids[:, None] == frame_ids[None, :])
        states = (inputs.astype(jnp.float32) + blocked_sum(((context, weights[0, 3]),))).astype(jnp.bfloat16)
        state_normed = layer_norm(states.astype(jnp.float32), norm_gains[2], norm_biases[2]).astype(jnp.bfloat16)
        token_normed = layer_norm(tokens_group[micro_index].astype(jnp.float32), norm_gains[1], norm_biases[1]).astype(jnp.bfloat16)
        dec_queries = project(token_normed, weights[1, 0])
        dec_keys = project(state_normed, weights[1, 1])
        dec_values = project(state_normed, weights[1, 2])
        dec_context, dec_probs = attend(dec_queries, dec_keys, dec_values, token_ids[:, None] == frame_ids[None, :])
        upstream = upstream_group[micro_index]
        grad_context = project(upstream, weights[1, 3])
        dec_key_grad, dec_value_grad = attend_backward(dec_queries, dec_keys, dec_values, dec_probs, grad_context)
        decoder_sum = decoder_sum + jnp.stack([outer_rows(dec_key_grad, state_normed), outer_rows(dec_value_grad, state_normed), outer_rows(dec_context, upstream)])
        grad_normed = blocked_sum(((dec_key_grad, weights[1, 1]), (dec_value_grad, weights[1, 2])))
        states_grad = norm_backward(grad_normed, states.astype(jnp.float32), norm_gains[2]).astype(jnp.bfloat16)
        att_grad = project(states_grad, weights[0, 3])
        enc_key_grad, enc_value_grad = attend_backward(queries, key_rows, value_rows, attn_probs, att_grad)
        encoder_sum = encoder_sum + jnp.stack([outer_rows(enc_key_grad, normed), outer_rows(enc_value_grad, normed), outer_rows(context, states_grad)])
    return jnp.stack([encoder_sum, decoder_sum]).astype(jnp.bfloat16)

def reference(frames, dec_states, out_grad, frame_lengths, token_lengths, weights, norm_gains, norm_biases):
    frames_split = frames.reshape(MB, N_DP, FRM, D).transpose(1, 0, 2, 3)
    tokens_split = dec_states.reshape(MB, N_DP, TKM, D).transpose(1, 0, 2, 3)
    upstream_split = out_grad.reshape(MB, N_DP, TKM, D).transpose(1, 0, 2, 3)
    frame_lens = frame_lengths.transpose(1, 0, 2)
    token_lens = token_lengths.transpose(1, 0, 2)

    def accumulate(running, group_items):
        group = group_terms(group_items[0], group_items[1], group_items[2], group_items[3], group_items[4], weights, norm_gains, norm_biases)
        return (running + lax.optimization_barrier(group).astype(jnp.float32), None)
    running, _ = lax.scan(accumulate, jnp.zeros((2, 3, HD, D), jnp.float32), (frames_split, tokens_split, upstream_split, frame_lens, token_lens))
    return running
```

```python
import functools
import math

import jax
import jax.numpy as jnp
from jax import lax
from jax.experimental import pallas as pl
from jax.experimental.pallas import tpu as pltpu
from jax.sharding import PartitionSpec as P

HS = 64
EPSILON = 1e-05
MESH = pl.DeviceIdType.MESH
F32 = jnp.float32
BF16 = jnp.bfloat16
NEAR = 2
CHUNKS = 4


def layer_norm(values, norm_gain, offset):
    center = values - jnp.mean(values, axis=-1, keepdims=True)
    variance = jnp.mean(center * center, axis=-1, keepdims=True)
    return center * lax.rsqrt(variance + EPSILON) * norm_gain + offset


def norm_backward(grad_out, values, norm_gain):
    center = values - jnp.mean(values, axis=-1, keepdims=True)
    variance = jnp.mean(center * center, axis=-1, keepdims=True)
    inverse = lax.rsqrt(variance + EPSILON)
    normed = center * inverse
    scaled = grad_out * norm_gain
    return inverse * (
        scaled
        - jnp.mean(scaled, axis=-1, keepdims=True)
        - normed * jnp.mean(scaled * normed, axis=-1, keepdims=True)
    )


def utterance_ids(lengths, row_count):
    bounds = jnp.cumsum(lengths, dtype=jnp.int32)
    places = jnp.arange(row_count, dtype=jnp.int32)
    return jnp.sum((places[:, None] >= bounds[None, :]).astype(jnp.int32), axis=1)


def project(row_block, matrix):
    return lax.dot_general(
        row_block, matrix, (((1,), (1,)), ((), ())), preferred_element_type=F32
    ).astype(BF16)


def outer_rows(left_rows, right_rows):
    return lax.dot_general(
        left_rows, right_rows, (((0,), (0,)), ((), ())), preferred_element_type=F32
    )


def split_heads(row_block):
    return row_block.reshape(row_block.shape[0], -1, HS)


def attend(queries, key_rows, value_rows, allowed):
    scaling = 1.0 / math.sqrt(HS)
    scores = (
        jnp.einsum(
            "qhd,khd->hqk", split_heads(queries), split_heads(key_rows), preferred_element_type=F32
        )
        * scaling
    )
    scores = jnp.where(allowed[None], scores, -1e30)
    highest = jnp.max(scores, axis=-1, keepdims=True)
    raised = jnp.exp(scores - highest)
    probs = raised * (1.0 / jnp.sum(raised, axis=-1, keepdims=True))
    probs = probs.astype(BF16)
    context = jnp.einsum("hqk,khd->qhd", probs, split_heads(value_rows), preferred_element_type=F32)
    return (context.reshape(queries.shape[0], -1).astype(BF16), probs)


def attend_backward(queries, value_rows, probs, grad_context):
    scaling = 1.0 / math.sqrt(HS)
    grad_heads = split_heads(grad_context)
    row_count = value_rows.shape[0]
    grad_probs = jnp.einsum(
        "qhd,khd->hqk", grad_heads, split_heads(value_rows), preferred_element_type=F32
    )
    wide = probs.astype(F32)
    grad_scores = (
        wide * (grad_probs - jnp.sum(grad_probs * wide, axis=-1, keepdims=True))
    ).astype(BF16)
    key_grad = (
        jnp.einsum("hqk,qhd->khd", grad_scores, split_heads(queries), preferred_element_type=F32)
        * scaling
    )
    value_grad = jnp.einsum("hqk,qhd->khd", probs, grad_heads, preferred_element_type=F32)
    return (
        key_grad.reshape(row_count, -1).astype(BF16),
        value_grad.reshape(row_count, -1).astype(BF16),
    )


def sum_kernel(
    near, far, chunks, g_ref, out_ref, near_in, held, far_in,
    near_send, near_recv, far_send, far_recv, back_send, back_recv, last_send, last_recv,
):
    me = lax.axis_index("dp")
    b = lax.rem(me, near)
    a = lax.div(me, near)
    other = a * near + (1 - b)

    def far_peer(apart):
        return lax.rem(a + apart, far) * near + b

    barrier = pltpu.get_barrier_semaphore()
    pl.semaphore_signal(barrier, inc=1, device_id={"dp": other}, device_id_type=MESH)
    for apart in range(1, far):
        pl.semaphore_signal(barrier, inc=1, device_id={"dp": far_peer(apart)}, device_id_type=MESH)
    pl.semaphore_wait(barrier, far)

    def near_copy(k):
        return pltpu.make_async_remote_copy(
            src_ref=g_ref.at[k, 1 - b],
            dst_ref=near_in.at[k],
            send_sem=near_send.at[k],
            recv_sem=near_recv.at[k],
            device_id={"dp": other},
            device_id_type=MESH,
        )

    def far_copy(k, apart):
        return pltpu.make_async_remote_copy(
            src_ref=held.at[k, lax.rem(a + apart, far)],
            dst_ref=far_in.at[k, apart - 1],
            send_sem=far_send.at[k, apart - 1],
            recv_sem=far_recv.at[k, apart - 1],
            device_id={"dp": far_peer(apart)},
            device_id_type=MESH,
        )

    def back_copy(k, apart):
        return pltpu.make_async_remote_copy(
            src_ref=out_ref.at[k, b, a],
            dst_ref=out_ref.at[k, b, a],
            send_sem=back_send.at[k, apart - 1],
            recv_sem=back_recv.at[k, apart - 1],
            device_id={"dp": far_peer(apart)},
            device_id_type=MESH,
        )

    def last_copy(k):
        return pltpu.make_async_remote_copy(
            src_ref=out_ref.at[k, b],
            dst_ref=out_ref.at[k, b],
            send_sem=last_send.at[k],
            recv_sem=last_recv.at[k],
            device_id={"dp": other},
            device_id_type=MESH,
        )

    def step_far(k):
        near_copy(k).wait_recv()
        held[k] = (g_ref[k, b].astype(F32) + near_in[k].astype(F32)).astype(BF16)
        for apart in range(1, far):
            far_copy(k, apart).start()

    def step_back(k):
        total = held[k, a].astype(F32)
        for apart in range(1, far):
            far_copy(k, apart).wait_recv()
            total = total + far_in[k, apart - 1].astype(F32)
        out_ref[k, b, a] = total.astype(BF16)
        for apart in range(1, far):
            back_copy(k, apart).start()

    def step_last(k):
        for apart in range(1, far):
            back_copy(k, apart).wait_recv()
        last_copy(k).start()

    for k in range(chunks):
        near_copy(k).start()
    for tick in range(chunks + 2):
        if tick < chunks:
            step_far(tick)
        if 0 <= tick - 1 < chunks:
            step_back(tick - 1)
        if 0 <= tick - 2 < chunks:
            step_last(tick - 2)
    for k in range(chunks):
        last_copy(k).wait_recv()
        near_copy(k).wait_send()
        last_copy(k).wait_send()
        for apart in range(1, far):
            far_copy(k, apart).wait_send()
            back_copy(k, apart).wait_send()


def sum_over_groups(terms):
    near = NEAR
    far = lax.axis_size("dp") // near
    rows, features = terms.shape
    unit = CHUNKS * near * far * 16
    padded = -(-rows // unit) * unit
    if padded != rows:
        terms = jnp.pad(terms, ((0, padded - rows), (0, 0)))
    piece = padded // (CHUNKS * near * far)
    blocks = terms.reshape(CHUNKS, near, far, piece, features)
    dma = pltpu.SemaphoreType.DMA
    out = pl.pallas_call(
        functools.partial(sum_kernel, near, far, CHUNKS),
        out_shape=jax.ShapeDtypeStruct(blocks.shape, BF16),
        in_specs=[pl.BlockSpec(memory_space=pltpu.VMEM)],
        out_specs=pl.BlockSpec(memory_space=pltpu.VMEM),
        scratch_shapes=[
            pltpu.VMEM((CHUNKS, far, piece, features), BF16),
            pltpu.VMEM((CHUNKS, far, piece, features), BF16),
            pltpu.VMEM((CHUNKS, far - 1, piece, features), BF16),
            dma((CHUNKS,)),
            dma((CHUNKS,)),
            dma((CHUNKS, far - 1)),
            dma((CHUNKS, far - 1)),
            dma((CHUNKS, far - 1)),
            dma((CHUNKS, far - 1)),
            dma((CHUNKS,)),
            dma((CHUNKS,)),
        ],
        compiler_params=pltpu.CompilerParams(
            collective_id=0, has_side_effects=True, vmem_limit_bytes=40 * 1024 * 1024
        ),
    )(blocks)
    return out.reshape(padded, features)[:rows]


def hop(values, source, target, apart):
    parts = lax.axis_size("mp")
    pairs = [(source * parts + i, target * parts + (i + apart) % parts) for i in range(parts)]
    return lax.ppermute(values, ("segment", "mp"), pairs)


def shards(
    frames, dec_states, out_grad, frame_lengths, token_lengths, weights, norm_gains, norm_biases
):
    is_encoder = lax.axis_index("segment") == 0
    matrices = weights[0]
    micro_count, shard_rows, features = frames.shape
    head_cols = matrices.shape[1]
    parts = lax.axis_size("mp")
    place = lax.axis_index("mp")
    frame_count = shard_rows * parts
    token_count = dec_states.shape[1]
    micros = range(micro_count)

    inputs = []
    for m in micros:
        full = jnp.zeros((frame_count, features), BF16)
        for apart in range(parts):
            if apart == 0:
                block = frames[m]
            else:
                block = hop(frames[m], 0, 0, apart)
                block = jnp.where(is_encoder, block, hop(block, 0, 1, 0))
            start = ((place - apart) % parts) * shard_rows
            full = lax.dynamic_update_slice(full, block, (start, 0))
        inputs.append(full)

    frame_ids = [utterance_ids(frame_lengths[m, 0], frame_count) for m in micros]
    token_ids = [utterance_ids(token_lengths[m, 0], token_count) for m in micros]

    enc = []
    sums = []
    for m in micros:
        normed = layer_norm(inputs[m].astype(F32), norm_gains[0], norm_biases[0]).astype(BF16)
        queries, key_rows, value_rows = [project(normed, matrices[i]) for i in range(3)]
        context, probs = attend(
            queries, key_rows, value_rows, frame_ids[m][:, None] == frame_ids[m][None, :]
        )
        partial = jnp.dot(context, matrices[3], preferred_element_type=F32).astype(BF16)
        enc.append((normed, queries, value_rows, context, probs))
        pieces = [hop(partial, 0, 1, apart) for apart in range(parts)]
        total = pieces[0].astype(F32)
        for apart in range(1, parts):
            total = total + pieces[apart].astype(F32)
        sums.append((inputs[m].astype(F32) + total).astype(BF16))

    upstream = out_grad.reshape(micro_count * token_count, features)
    tokens = dec_states.reshape(micro_count * token_count, features)
    token_normed = layer_norm(tokens.astype(F32), norm_gains[1], norm_biases[1]).astype(BF16)
    dec_queries = project(token_normed, matrices[0])
    grad_context = project(upstream, matrices[3])
    states = [hop(rows, 1, 0, 0) for rows in sums]
    dec = []
    backs = []
    for m in micros:
        rows = slice(m * token_count, (m + 1) * token_count)
        normed = layer_norm(sums[m].astype(F32), norm_gains[2], norm_biases[2]).astype(BF16)
        key_rows, value_rows = [project(normed, matrices[i]) for i in (1, 2)]
        context, probs = attend(
            dec_queries[rows], key_rows, value_rows, token_ids[m][:, None] == frame_ids[m][None, :]
        )
        key_grad, value_grad = attend_backward(
            dec_queries[rows], value_rows, probs, grad_context[rows]
        )
        partial = (
            jnp.dot(key_grad, matrices[1], preferred_element_type=F32)
            + jnp.dot(value_grad, matrices[2], preferred_element_type=F32)
        ).astype(BF16)
        dec.append((normed, key_grad, value_grad, context))
        total = hop(partial, 1, 0, 0).astype(F32)
        for apart in range(1, parts):
            total = total + hop(partial, 1, 0, apart).astype(F32)
        backs.append(total)

    def joined(items, index):
        return jnp.concatenate([item[index] for item in items], axis=0)

    dec_normed = joined(dec, 0)
    dec_terms = jnp.concatenate(
        [
            outer_rows(joined(dec, 1), dec_normed).astype(BF16),
            outer_rows(joined(dec, 2), dec_normed).astype(BF16),
            outer_rows(joined(dec, 3), upstream).astype(BF16),
        ],
        axis=0,
    )

    def encoder_back():
        grads = []
        state_grads = []
        for m in micros:
            _, queries, value_rows, _, probs = enc[m]
            state_grad = norm_backward(backs[m], states[m].astype(F32), norm_gains[2]).astype(BF16)
            state_grads.append(state_grad)
            grads.append(
                attend_backward(queries, value_rows, probs, project(state_grad, matrices[3]))
            )
        normed = joined(enc, 0)
        return jnp.concatenate(
            [
                outer_rows(joined(grads, 0), normed).astype(BF16),
                outer_rows(joined(grads, 1), normed).astype(BF16),
                outer_rows(joined(enc, 3), jnp.concatenate(state_grads, axis=0)).astype(BF16),
            ],
            axis=0,
        )

    terms = lax.cond(is_encoder, encoder_back, lambda: dec_terms)
    gradient = sum_over_groups(terms).astype(F32)
    return gradient.reshape(1, 3, head_cols, features)


def solution(mesh):
    placed = (
        P(None, ("dp", "mp"), None),
        P(None, "dp", None),
        P(None, "dp", None),
        P(None, "dp", None),
        P(None, "dp", None),
        P("segment", None, "mp", None),
        P(),
        P(),
    )
    return jax.shard_map(
        shards,
        mesh=mesh,
        in_specs=placed,
        out_specs=P("segment", None, "mp", None),
        check_vma=False,
    )
```

```python
import functools
import math

import jax
import jax.numpy as jnp
from jax import lax
from jax.experimental import pallas as pl
from jax.experimental.pallas import tpu as pltpu
from jax.sharding import PartitionSpec as P

HS = 64
EPSILON = 1e-05
MESH = pl.DeviceIdType.MESH
F32 = jnp.float32
BF16 = jnp.bfloat16
NEAR = 2
CHUNKS = 4


def dot_rows(left, right):
    return lax.dot_general(left, right, (((1,), (1,)), ((), ())), preferred_element_type=F32)


def dot_plain(left, right):
    return lax.dot_general(left, right, (((1,), (0,)), ((), ())), preferred_element_type=F32)


def dot_outer(left, right):
    return lax.dot_general(left, right, (((0,), (0,)), ((), ())), preferred_element_type=F32)


def standardize(values):
    center = values - jnp.mean(values, axis=-1, keepdims=True)
    inverse = lax.rsqrt(jnp.mean(center * center, axis=-1, keepdims=True) + EPSILON)
    return center * inverse, inverse


def flat(rows):
    return rows.reshape(rows.shape[0] * rows.shape[1], rows.shape[2])


def utterance_ids(lengths_ref, m, shape, dim):
    places = lax.broadcasted_iota(jnp.int32, shape, dim)
    ids = jnp.zeros(shape, jnp.int32)
    bound = jnp.int32(0)
    for utterance in range(lengths_ref.shape[1]):
        bound = bound + lengths_ref[m, utterance]
        ids = ids + jnp.where(places >= bound, 1, 0)
    return ids


def mask_bias(frame_lens, other_lens, m, frame_count, other_count):
    shape = (frame_count, other_count)
    same = utterance_ids(frame_lens, m, shape, 0) == utterance_ids(other_lens, m, shape, 1)
    return jnp.where(same, 0.0, -1e30).astype(F32)


def head_probs(key_rows, queries, bias):
    scores = dot_rows(key_rows, queries) + bias
    raised = jnp.exp(scores - jnp.max(scores, axis=0, keepdims=True))
    return raised * (1.0 / jnp.sum(raised, axis=0, keepdims=True))


def head_scores_grad(probs, value_rows, grad_rows):
    grad_probs = dot_rows(value_rows, grad_rows)
    return (probs * (grad_probs - jnp.sum(grad_probs * probs, axis=0, keepdims=True))).astype(BF16)


def section_kernel(
    parts, frame_lens, token_lens, frames, tokens, upstream, weights, gains, biases, terms,
    full, normed, queries, key_rows, value_rows, context, probs, part, inbox, states, state_grad,
    key_grad, value_grad, bias, dec_bias, dec_queries, dec_grad, dec_context,
    frame_send, frame_recv, pass_send, pass_recv, part_send, part_recv, state_send, state_recv,
):
    section = lax.axis_index("segment")
    place = lax.axis_index("mp")
    micro_count, shard_rows, features = frames.shape
    frame_count = shard_rows * parts
    token_count = tokens.shape[1]
    head_cols = weights.shape[1]
    heads = head_cols // HS
    scaling = 1.0 / math.sqrt(HS)

    barrier = pltpu.get_barrier_semaphore()
    for apart in range(parts):
        for side in range(2):
            if apart == 0 and side == 0:
                continue
            pl.semaphore_signal(
                barrier,
                inc=1,
                device_id={
                    "segment": lax.rem(section + side, 2),
                    "mp": lax.rem(place + apart, parts),
                },
                device_id_type=MESH,
            )
    pl.semaphore_wait(barrier, 2 * parts - 1)

    def copy_to(source, target, sends, recvs, side, apart):
        return pltpu.make_async_remote_copy(
            src_ref=source,
            dst_ref=target,
            send_sem=sends,
            recv_sem=recvs,
            device_id={"segment": side, "mp": lax.rem(place + apart, parts)},
            device_id_type=MESH,
        )

    def frame_copy(m, apart):
        return copy_to(
            frames.at[m], full.at[m, place], frame_send.at[m, apart], frame_recv.at[m, apart],
            0, apart,
        )

    def pass_copy(m, apart):
        origin = lax.rem(place - apart + parts, parts)
        return copy_to(
            full.at[m, origin], full.at[m, origin], pass_send.at[m, apart],
            pass_recv.at[m, apart], 1, 0,
        )

    def part_copy(m, apart, side):
        return copy_to(
            part.at[m], inbox.at[m, apart], part_send.at[m, apart], part_recv.at[m, apart],
            side, apart,
        )

    def state_copy(m):
        return copy_to(states.at[m], states.at[m], state_send.at[m], state_recv.at[m], 0, 0)

    def send_parts(m, side):
        for apart in range(1, parts):
            part_copy(m, apart, side).start()
        part_copy(m, 0, side).start()

    def received_sum(m, side):
        total = None
        for apart in range(parts):
            part_copy(m, apart, side).wait_recv()
            piece = inbox[m, apart].astype(F32)
            total = piece if total is None else total + piece
        return total

    def store_terms(last_left, last_right):
        block = min(256, head_cols)
        sources = ((key_grad, normed), (value_grad, normed), (last_left, last_right))
        for index, (left, right) in enumerate(sources):
            wide = flat(right[...])
            for start in range(0, head_cols, block):
                columns = slice(start, start + block)
                terms[index, columns, :] = dot_outer(flat(left[:, :, columns]), wide).astype(BF16)

    def encoder_forward(m, carry):
        for apart in range(1, parts):
            frame_copy(m, apart).wait_recv()
        for apart in range(1, parts):
            pass_copy(m, apart).start()
        rows, _ = standardize(flat(full[m]).astype(F32))
        normed[m] = (rows * gains[0:1, :] + biases[0:1, :]).astype(BF16)
        row_input = normed[m]
        queries[m] = (dot_rows(row_input, weights[0]).astype(BF16) * scaling).astype(BF16)
        key_rows[m] = dot_rows(row_input, weights[1]).astype(BF16)
        value_rows[m] = dot_rows(row_input, weights[2]).astype(BF16)
        bias[...] = mask_bias(frame_lens, frame_lens, m, frame_count, frame_count)
        for h in range(heads):
            cols = slice(h * HS, (h + 1) * HS)
            head = head_probs(key_rows[m, :, cols], queries[m, :, cols], bias[...]).astype(BF16)
            probs[m, h] = head
            context[m, :, cols] = dot_outer(head, value_rows[m, :, cols]).astype(BF16)
        part[m] = dot_plain(context[m], weights[3]).astype(BF16)
        send_parts(m, 1)
        return carry

    def encoder_backward(m, carry):
        grad_out = received_sum(m, 0)
        state_copy(m).wait_recv()
        rows, inverse = standardize(states[m].astype(F32))
        scaled = grad_out * gains[2:3, :]
        state_grad[m] = (
            inverse
            * (
                scaled
                - jnp.mean(scaled, axis=-1, keepdims=True)
                - rows * jnp.mean(scaled * rows, axis=-1, keepdims=True)
            )
        ).astype(BF16)
        grad_rows = dot_rows(state_grad[m], weights[3]).astype(BF16)
        key_rows[m] = grad_rows
        for h in range(heads):
            cols = slice(h * HS, (h + 1) * HS)
            grad_head = key_rows[m, :, cols]
            head = probs[m, h]
            change = head_scores_grad(head.astype(F32), value_rows[m, :, cols], grad_head)
            key_grad[m, :, cols] = dot_plain(change, queries[m, :, cols]).astype(BF16)
            value_grad[m, :, cols] = dot_plain(head, grad_head).astype(BF16)
        return carry

    def decoder_step(m, carry):
        for apart in range(1, parts):
            pass_copy(m, apart).wait_recv()
        total = received_sum(m, 1)
        states[m] = (flat(full[m]).astype(F32) + total).astype(BF16)
        state_copy(m).start()
        rows, _ = standardize(states[m].astype(F32))
        normed[m] = (rows * gains[2:3, :] + biases[2:3, :]).astype(BF16)
        row_input = normed[m]
        key_rows[m] = dot_rows(row_input, weights[1]).astype(BF16)
        value_rows[m] = dot_rows(row_input, weights[2]).astype(BF16)
        dec_bias[...] = mask_bias(frame_lens, token_lens, m, frame_count, token_count)
        for h in range(heads):
            cols = slice(h * HS, (h + 1) * HS)
            query_head = dec_queries[m, :, cols]
            value_head = value_rows[m, :, cols]
            grad_head = dec_grad[m, :, cols]
            exact = head_probs(key_rows[m, :, cols], query_head, dec_bias[...])
            head = exact.astype(BF16)
            dec_context[m, :, cols] = dot_outer(head, value_head).astype(BF16)
            change = head_scores_grad(exact, value_head, grad_head)
            key_grad[m, :, cols] = dot_plain(change, query_head).astype(BF16)
            value_grad[m, :, cols] = dot_plain(head, grad_head).astype(BF16)
        part[m] = (
            dot_plain(key_grad[m], weights[1]) + dot_plain(value_grad[m], weights[2])
        ).astype(BF16)
        send_parts(m, 0)
        return carry

    @pl.when(section == 0)
    def _():
        for m in range(micro_count):
            for apart in range(1, parts):
                frame_copy(m, apart).start()
        for m in range(micro_count):
            full[m, place] = frames[m]
        lax.fori_loop(0, micro_count, encoder_forward, 0)
        lax.fori_loop(0, micro_count, encoder_backward, 0)
        store_terms(context, state_grad)
        for m in range(micro_count):
            for apart in range(1, parts):
                frame_copy(m, apart).wait_send()
                pass_copy(m, apart).wait_send()
            for apart in range(parts):
                part_copy(m, apart, 1).wait_send()

    @pl.when(section == 1)
    def _():
        for m in range(micro_count):
            full[m, place] = frames[m]
        rows, _ = standardize(flat(tokens[...]).astype(F32))
        token_rows = (rows * gains[1:2, :] + biases[1:2, :]).astype(BF16)
        small = (micro_count, token_count, head_cols)
        token_queries = dot_rows(token_rows, weights[0]).astype(BF16) * scaling
        dec_queries[...] = token_queries.astype(BF16).reshape(small)
        dec_grad[...] = dot_rows(flat(upstream[...]), weights[3]).astype(BF16).reshape(small)
        lax.fori_loop(0, micro_count, decoder_step, 0)
        store_terms(dec_context, upstream)
        for m in range(micro_count):
            state_copy(m).wait_send()
            for apart in range(parts):
                part_copy(m, apart, 0).wait_send()


def section_terms(
    frames, dec_states, out_grad, frame_lengths, token_lengths, matrices, norm_gains, norm_biases
):
    parts = lax.axis_size("mp")
    micro_count, shard_rows, features = frames.shape
    frame_count = shard_rows * parts
    token_count = dec_states.shape[1]
    head_cols = matrices.shape[1]
    dma = pltpu.SemaphoreType.DMA
    wide = pltpu.VMEM((micro_count, frame_count, features), BF16)
    thin = pltpu.VMEM((micro_count, frame_count, head_cols), BF16)
    small = pltpu.VMEM((micro_count, token_count, head_cols), BF16)
    pairs = dma((micro_count, parts))
    return pl.pallas_call(
        functools.partial(section_kernel, parts),
        out_shape=jax.ShapeDtypeStruct((3, head_cols, features), BF16),
        in_specs=[pl.BlockSpec(memory_space=pltpu.SMEM)] * 2
        + [pl.BlockSpec(memory_space=pltpu.VMEM)] * 6,
        out_specs=pl.BlockSpec(memory_space=pltpu.VMEM),
        scratch_shapes=[
            pltpu.VMEM((micro_count, parts, shard_rows, features), BF16),
            wide,
            thin,
            thin,
            thin,
            thin,
            pltpu.VMEM((micro_count, head_cols // HS, frame_count, frame_count), BF16),
            wide,
            pltpu.VMEM((micro_count, parts, frame_count, features), BF16),
            wide,
            wide,
            thin,
            thin,
            pltpu.VMEM((frame_count, frame_count), F32),
            pltpu.VMEM((frame_count, token_count), F32),
            small,
            small,
            small,
            pairs,
            pairs,
            pairs,
            pairs,
            pairs,
            pairs,
            dma((micro_count,)),
            dma((micro_count,)),
        ],
        compiler_params=pltpu.CompilerParams(
            collective_id=1, has_side_effects=True, vmem_limit_bytes=52 * 1024 * 1024
        ),
    )(
        frame_lengths[:, 0], token_lengths[:, 0], frames, dec_states, out_grad, matrices,
        norm_gains, norm_biases,
    )


def sum_kernel(
    near, far, chunks, g_ref, out_ref, near_in, held, far_in,
    near_send, near_recv, far_send, far_recv, back_send, back_recv, last_send, last_recv,
):
    me = lax.axis_index("dp")
    b = lax.rem(me, near)
    a = lax.div(me, near)
    other = a * near + (1 - b)

    def far_peer(apart):
        return lax.rem(a + apart, far) * near + b

    barrier = pltpu.get_barrier_semaphore()
    pl.semaphore_signal(barrier, inc=1, device_id={"dp": other}, device_id_type=MESH)
    for apart in range(1, far):
        pl.semaphore_signal(barrier, inc=1, device_id={"dp": far_peer(apart)}, device_id_type=MESH)
    pl.semaphore_wait(barrier, far)

    def near_copy(k):
        return pltpu.make_async_remote_copy(
            src_ref=g_ref.at[k, 1 - b],
            dst_ref=near_in.at[k],
            send_sem=near_send.at[k],
            recv_sem=near_recv.at[k],
            device_id={"dp": other},
            device_id_type=MESH,
        )

    def far_copy(k, apart):
        return pltpu.make_async_remote_copy(
            src_ref=held.at[k, lax.rem(a + apart, far)],
            dst_ref=far_in.at[k, apart - 1],
            send_sem=far_send.at[k, apart - 1],
            recv_sem=far_recv.at[k, apart - 1],
            device_id={"dp": far_peer(apart)},
            device_id_type=MESH,
        )

    def back_copy(k, apart):
        return pltpu.make_async_remote_copy(
            src_ref=out_ref.at[k, b, a],
            dst_ref=out_ref.at[k, b, a],
            send_sem=back_send.at[k, apart - 1],
            recv_sem=back_recv.at[k, apart - 1],
            device_id={"dp": far_peer(apart)},
            device_id_type=MESH,
        )

    def last_copy(k):
        return pltpu.make_async_remote_copy(
            src_ref=out_ref.at[k, b],
            dst_ref=out_ref.at[k, b],
            send_sem=last_send.at[k],
            recv_sem=last_recv.at[k],
            device_id={"dp": other},
            device_id_type=MESH,
        )

    def step_far(k):
        near_copy(k).wait_recv()
        if k + 2 < chunks:
            near_copy(k + 2).start()
        held[k] = (g_ref[k, b].astype(F32) + near_in[k].astype(F32)).astype(BF16)
        for apart in range(1, far):
            far_copy(k, apart).start()

    def step_back(k):
        total = held[k, a].astype(F32)
        for apart in range(1, far):
            far_copy(k, apart).wait_recv()
            total = total + far_in[k, apart - 1].astype(F32)
        out_ref[k, b, a] = total.astype(BF16)
        for apart in range(1, far):
            back_copy(k, apart).start()

    def step_last(k):
        for apart in range(1, far):
            back_copy(k, apart).wait_recv()
        last_copy(k).start()

    for k in range(min(2, chunks)):
        near_copy(k).start()
    for tick in range(chunks + 2):
        if tick < chunks:
            step_far(tick)
        if 0 <= tick - 1 < chunks:
            step_back(tick - 1)
        if 0 <= tick - 2 < chunks:
            step_last(tick - 2)
    for k in range(chunks):
        last_copy(k).wait_recv()
        near_copy(k).wait_send()
        last_copy(k).wait_send()
        for apart in range(1, far):
            far_copy(k, apart).wait_send()
            back_copy(k, apart).wait_send()


def sum_over_groups(terms):
    near = NEAR
    far = lax.axis_size("dp") // near
    rows, features = terms.shape
    unit = CHUNKS * near * far * 16
    padded = -(-rows // unit) * unit
    if padded != rows:
        terms = jnp.pad(terms, ((0, padded - rows), (0, 0)))
    piece = padded // (CHUNKS * near * far)
    blocks = terms.reshape(CHUNKS, near, far, piece, features)
    dma = pltpu.SemaphoreType.DMA
    out = pl.pallas_call(
        functools.partial(sum_kernel, near, far, CHUNKS),
        out_shape=jax.ShapeDtypeStruct(blocks.shape, BF16),
        in_specs=[pl.BlockSpec(memory_space=pltpu.VMEM)],
        out_specs=pl.BlockSpec(memory_space=pltpu.VMEM),
        scratch_shapes=[
            pltpu.VMEM((CHUNKS, far, piece, features), BF16),
            pltpu.VMEM((CHUNKS, far, piece, features), BF16),
            pltpu.VMEM((CHUNKS, far - 1, piece, features), BF16),
            dma((CHUNKS,)),
            dma((CHUNKS,)),
            dma((CHUNKS, far - 1)),
            dma((CHUNKS, far - 1)),
            dma((CHUNKS, far - 1)),
            dma((CHUNKS, far - 1)),
            dma((CHUNKS,)),
            dma((CHUNKS,)),
        ],
        compiler_params=pltpu.CompilerParams(
            collective_id=0, has_side_effects=True, vmem_limit_bytes=40 * 1024 * 1024
        ),
    )(blocks)
    return out.reshape(padded, features)[:rows]


def shards(
    frames, dec_states, out_grad, frame_lengths, token_lengths, weights, norm_gains, norm_biases
):
    matrices = weights[0]
    head_cols, features = matrices.shape[1:]
    terms = section_terms(
        frames, dec_states, out_grad, frame_lengths, token_lengths, matrices, norm_gains,
        norm_biases,
    )
    gradient = sum_over_groups(terms.reshape(3 * head_cols, features)).astype(F32)
    return gradient.reshape(1, 3, head_cols, features)


def solution(mesh):
    placed = (
        P(None, ("dp", "mp"), None),
        P(None, "dp", None),
        P(None, "dp", None),
        P(None, "dp", None),
        P(None, "dp", None),
        P("segment", None, "mp", None),
        P(),
        P(),
    )
    return jax.shard_map(
        shards,
        mesh=mesh,
        in_specs=placed,
        out_specs=P("segment", None, "mp", None),
        check_vma=False,
    )
```

```python
import functools
import math

import jax
import jax.numpy as jnp
from jax import lax
from jax.experimental import pallas as pl
from jax.experimental.pallas import tpu as pltpu
from jax.sharding import PartitionSpec as P

HS = 64
EPSILON = 1e-05
MESH = pl.DeviceIdType.MESH
F32 = jnp.float32
BF16 = jnp.bfloat16
NEAR = 2
CUTS = 2


def dot_rows(left, right):
    return lax.dot_general(left, right, (((1,), (1,)), ((), ())), preferred_element_type=F32)


def dot_plain(left, right):
    return lax.dot_general(left, right, (((1,), (0,)), ((), ())), preferred_element_type=F32)


def dot_outer(left, right):
    return lax.dot_general(left, right, (((0,), (0,)), ((), ())), preferred_element_type=F32)


def standardize(values):
    center = values - jnp.mean(values, axis=-1, keepdims=True)
    inverse = lax.rsqrt(jnp.mean(center * center, axis=-1, keepdims=True) + EPSILON)
    return center * inverse, inverse


def flat(rows):
    return rows.reshape(rows.shape[0] * rows.shape[1], rows.shape[2])


def utterance_ids(lengths_ref, m, shape, dim):
    places = lax.broadcasted_iota(jnp.int32, shape, dim)
    ids = jnp.zeros(shape, jnp.int32)
    bound = jnp.int32(0)
    for utterance in range(lengths_ref.shape[1]):
        bound = bound + lengths_ref[m, utterance]
        ids = ids + jnp.where(places >= bound, 1, 0)
    return ids


def mask_bias(frame_lens, other_lens, m, frame_count, other_count):
    shape = (frame_count, other_count)
    same = utterance_ids(frame_lens, m, shape, 0) == utterance_ids(other_lens, m, shape, 1)
    return jnp.where(same, 0.0, -1e30).astype(F32)


def head_probs(key_rows, queries, bias):
    scores = dot_rows(key_rows, queries) + bias
    raised = jnp.exp(scores - jnp.max(scores, axis=0, keepdims=True))
    return raised * (1.0 / jnp.sum(raised, axis=0, keepdims=True))


def head_scores_grad(probs, value_rows, grad_rows):
    grad_probs = dot_rows(value_rows, grad_rows)
    return (probs * (grad_probs - jnp.sum(grad_probs * probs, axis=0, keepdims=True))).astype(BF16)


def section_kernel(
    parts, frame_lens, token_lens, frames, tokens, upstream, weights, gains, biases, terms,
    full, normed, queries, key_rows, value_rows, context, probs, part, inbox, states, state_grad,
    key_grad, value_grad, bias, dec_bias, dec_queries, dec_grad, dec_context,
    frame_send, frame_recv, pass_send, pass_recv, part_send, part_recv, state_send, state_recv,
):
    section = lax.axis_index("segment")
    place = lax.axis_index("mp")
    micro_count, shard_rows, features = frames.shape
    frame_count = shard_rows * parts
    token_count = tokens.shape[1]
    head_cols = weights.shape[1]
    heads = head_cols // HS
    scaling = 1.0 / math.sqrt(HS)

    barrier = pltpu.get_barrier_semaphore()
    for apart in range(parts):
        for side in range(2):
            if apart == 0 and side == 0:
                continue
            pl.semaphore_signal(
                barrier,
                inc=1,
                device_id={
                    "segment": lax.rem(section + side, 2),
                    "mp": lax.rem(place + apart, parts),
                },
                device_id_type=MESH,
            )
    pl.semaphore_wait(barrier, 2 * parts - 1)

    def copy_to(source, target, sends, recvs, side, apart):
        return pltpu.make_async_remote_copy(
            src_ref=source,
            dst_ref=target,
            send_sem=sends,
            recv_sem=recvs,
            device_id={"segment": side, "mp": lax.rem(place + apart, parts)},
            device_id_type=MESH,
        )

    def frame_copy(m, apart):
        return copy_to(
            frames.at[m], full.at[m, place], frame_send.at[m, apart], frame_recv.at[m, apart],
            0, apart,
        )

    def pass_copy(m, apart):
        origin = lax.rem(place - apart + parts, parts)
        return copy_to(
            full.at[m, origin], full.at[m, origin], pass_send.at[m, apart],
            pass_recv.at[m, apart], 1, 0,
        )

    def part_copy(m, apart, side):
        return copy_to(
            part.at[m], inbox.at[m, apart], part_send.at[m, apart], part_recv.at[m, apart],
            side, apart,
        )

    def state_copy(m):
        return copy_to(states.at[m], states.at[m], state_send.at[m], state_recv.at[m], 0, 0)

    def send_parts(m, side):
        for apart in range(1, parts):
            part_copy(m, apart, side).start()
        part_copy(m, 0, side).start()

    def received_sum(m, side):
        total = None
        for apart in range(parts):
            part_copy(m, apart, side).wait_recv()
            piece = inbox[m, apart].astype(F32)
            total = piece if total is None else total + piece
        return total

    def store_terms(last_left, last_right):
        block = min(256, head_cols)
        sources = ((key_grad, normed), (value_grad, normed), (last_left, last_right))
        for index, (left, right) in enumerate(sources):
            wide = flat(right[...])
            for start in range(0, head_cols, block):
                columns = slice(start, start + block)
                terms[index, columns, :] = dot_outer(flat(left[:, :, columns]), wide).astype(BF16)

    def encoder_forward(m, carry):
        for apart in range(1, parts):
            frame_copy(m, apart).wait_recv()
        for apart in range(1, parts):
            pass_copy(m, apart).start()
        rows, _ = standardize(flat(full[m]).astype(F32))
        normed[m] = (rows * gains[0:1, :] + biases[0:1, :]).astype(BF16)
        row_input = normed[m]
        queries[m] = (dot_rows(row_input, weights[0]).astype(BF16) * scaling).astype(BF16)
        key_rows[m] = dot_rows(row_input, weights[1]).astype(BF16)
        value_rows[m] = dot_rows(row_input, weights[2]).astype(BF16)
        bias[...] = mask_bias(frame_lens, frame_lens, m, frame_count, frame_count)
        for h in range(heads):
            cols = slice(h * HS, (h + 1) * HS)
            head = head_probs(key_rows[m, :, cols], queries[m, :, cols], bias[...]).astype(BF16)
            probs[m, h] = head
            context[m, :, cols] = dot_outer(head, value_rows[m, :, cols]).astype(BF16)
        part[m] = dot_plain(context[m], weights[3]).astype(BF16)
        send_parts(m, 1)
        return carry

    def encoder_backward(m, carry):
        grad_out = received_sum(m, 0)
        state_copy(m).wait_recv()
        rows, inverse = standardize(states[m].astype(F32))
        scaled = grad_out * gains[2:3, :]
        state_grad[m] = (
            inverse
            * (
                scaled
                - jnp.mean(scaled, axis=-1, keepdims=True)
                - rows * jnp.mean(scaled * rows, axis=-1, keepdims=True)
            )
        ).astype(BF16)
        grad_rows = dot_rows(state_grad[m], weights[3]).astype(BF16)
        key_rows[m] = grad_rows
        for h in range(heads):
            cols = slice(h * HS, (h + 1) * HS)
            grad_head = key_rows[m, :, cols]
            head = probs[m, h]
            change = head_scores_grad(head.astype(F32), value_rows[m, :, cols], grad_head)
            key_grad[m, :, cols] = dot_plain(change, queries[m, :, cols]).astype(BF16)
            value_grad[m, :, cols] = dot_plain(head, grad_head).astype(BF16)
        return carry

    def decoder_step(m, carry):
        for apart in range(1, parts):
            pass_copy(m, apart).wait_recv()
        total = received_sum(m, 1)
        states[m] = (flat(full[m]).astype(F32) + total).astype(BF16)
        state_copy(m).start()
        rows, _ = standardize(states[m].astype(F32))
        normed[m] = (rows * gains[2:3, :] + biases[2:3, :]).astype(BF16)
        row_input = normed[m]
        key_rows[m] = dot_rows(row_input, weights[1]).astype(BF16)
        value_rows[m] = dot_rows(row_input, weights[2]).astype(BF16)
        dec_bias[...] = mask_bias(frame_lens, token_lens, m, frame_count, token_count)
        for h in range(heads):
            cols = slice(h * HS, (h + 1) * HS)
            query_head = dec_queries[m, :, cols]
            value_head = value_rows[m, :, cols]
            grad_head = dec_grad[m, :, cols]
            exact = head_probs(key_rows[m, :, cols], query_head, dec_bias[...])
            head = exact.astype(BF16)
            dec_context[m, :, cols] = dot_outer(head, value_head).astype(BF16)
            change = head_scores_grad(exact, value_head, grad_head)
            key_grad[m, :, cols] = dot_plain(change, query_head).astype(BF16)
            value_grad[m, :, cols] = dot_plain(head, grad_head).astype(BF16)
        part[m] = (
            dot_plain(key_grad[m], weights[1]) + dot_plain(value_grad[m], weights[2])
        ).astype(BF16)
        send_parts(m, 0)
        return carry

    @pl.when(section == 0)
    def _():
        for m in range(micro_count):
            for apart in range(1, parts):
                frame_copy(m, apart).start()
        for m in range(micro_count):
            full[m, place] = frames[m]
        lax.fori_loop(0, micro_count, encoder_forward, 0)
        lax.fori_loop(0, micro_count, encoder_backward, 0)
        store_terms(context, state_grad)
        for m in range(micro_count):
            for apart in range(1, parts):
                frame_copy(m, apart).wait_send()
                pass_copy(m, apart).wait_send()
            for apart in range(parts):
                part_copy(m, apart, 1).wait_send()

    @pl.when(section == 1)
    def _():
        for m in range(micro_count):
            full[m, place] = frames[m]
        rows, _ = standardize(flat(tokens[...]).astype(F32))
        token_rows = (rows * gains[1:2, :] + biases[1:2, :]).astype(BF16)
        small = (micro_count, token_count, head_cols)
        token_queries = dot_rows(token_rows, weights[0]).astype(BF16) * scaling
        dec_queries[...] = token_queries.astype(BF16).reshape(small)
        dec_grad[...] = dot_rows(flat(upstream[...]), weights[3]).astype(BF16).reshape(small)
        lax.fori_loop(0, micro_count, decoder_step, 0)
        store_terms(dec_context, upstream)
        for m in range(micro_count):
            state_copy(m).wait_send()
            for apart in range(parts):
                part_copy(m, apart, 0).wait_send()


def section_terms(
    frames, dec_states, out_grad, frame_lengths, token_lengths, matrices, norm_gains, norm_biases
):
    parts = lax.axis_size("mp")
    micro_count, shard_rows, features = frames.shape
    frame_count = shard_rows * parts
    token_count = dec_states.shape[1]
    head_cols = matrices.shape[1]
    dma = pltpu.SemaphoreType.DMA
    wide = pltpu.VMEM((micro_count, frame_count, features), BF16)
    thin = pltpu.VMEM((micro_count, frame_count, head_cols), BF16)
    small = pltpu.VMEM((micro_count, token_count, head_cols), BF16)
    pairs = dma((micro_count, parts))
    return pl.pallas_call(
        functools.partial(section_kernel, parts),
        out_shape=jax.ShapeDtypeStruct((3, head_cols, features), BF16),
        in_specs=[pl.BlockSpec(memory_space=pltpu.SMEM)] * 2
        + [pl.BlockSpec(memory_space=pltpu.VMEM)] * 6,
        out_specs=pl.BlockSpec(memory_space=pltpu.VMEM),
        scratch_shapes=[
            pltpu.VMEM((micro_count, parts, shard_rows, features), BF16),
            wide,
            thin,
            thin,
            thin,
            thin,
            pltpu.VMEM((micro_count, head_cols // HS, frame_count, frame_count), BF16),
            wide,
            pltpu.VMEM((micro_count, parts, frame_count, features), BF16),
            wide,
            wide,
            thin,
            thin,
            pltpu.VMEM((frame_count, frame_count), F32),
            pltpu.VMEM((frame_count, token_count), F32),
            small,
            small,
            small,
            pairs,
            pairs,
            pairs,
            pairs,
            pairs,
            pairs,
            dma((micro_count,)),
            dma((micro_count,)),
        ],
        compiler_params=pltpu.CompilerParams(
            collective_id=1, has_side_effects=True, vmem_limit_bytes=52 * 1024 * 1024
        ),
    )(
        frame_lengths[:, 0], token_lengths[:, 0], frames, dec_states, out_grad, matrices,
        norm_gains, norm_biases,
    )


def sum_kernel(
    size, cuts, g_ref, out_ref, held, inbox, add_send, add_recv, back_send, back_recv
):
    near = NEAR
    far = size // near
    me = lax.axis_index("dp")
    b = lax.rem(me, near)
    a = lax.div(me, near)
    place = jnp.where(b == 0, a, 2 * far - 1 - a)

    def device_at(spot):
        spot = lax.rem(spot + size, size)
        return jnp.where(spot < far, spot * near, (2 * far - 1 - spot) * near + 1)

    ways = (1, -1)
    peers = [device_at(place + way) for way in ways]

    barrier = pltpu.get_barrier_semaphore()
    for peer in peers:
        pl.semaphore_signal(barrier, inc=1, device_id={"dp": peer}, device_id_type=MESH)
    pl.semaphore_wait(barrier, 2)

    def block(d, apart):
        return lax.rem(place + ways[d] * apart + 2 * size, size)

    def add_copy(d, c, step, first):
        source = g_ref.at[d, c, block(d, 0)] if first else held.at[d, c, step - 1]
        return pltpu.make_async_remote_copy(
            src_ref=source,
            dst_ref=inbox.at[d, c, step],
            send_sem=add_send.at[d, c, step],
            recv_sem=add_recv.at[d, c, step],
            device_id={"dp": peers[d]},
            device_id_type=MESH,
        )

    def back_copy(d, c, step):
        ref = out_ref.at[d, c, block(d, 1 - step)]
        return pltpu.make_async_remote_copy(
            src_ref=ref,
            dst_ref=ref,
            send_sem=back_send.at[d, c, step],
            recv_sem=back_recv.at[d, c, step],
            device_id={"dp": peers[d]},
            device_id_type=MESH,
        )

    streams = [(d, c) for c in range(cuts) for d in range(2)]
    last = size - 2

    def summed(d, c, step):
        mine = g_ref[d, c, block(d, -step - 1)].astype(F32)
        return (mine + inbox[d, c, step].astype(F32)).astype(BF16)

    for d, c in streams:
        add_copy(d, c, 0, True).start()

    def add_step(step, carry):
        for d, c in streams:
            wait_add(d, c, step)
            held[d, c, step] = summed(d, c, step)
            add_copy(d, c, step + 1, False).start()
        return carry

    def wait_add(d, c, step):
        pltpu.make_async_remote_copy(
            src_ref=held.at[d, c, step],
            dst_ref=inbox.at[d, c, step],
            send_sem=add_send.at[d, c, step],
            recv_sem=add_recv.at[d, c, step],
            device_id={"dp": peers[d]},
            device_id_type=MESH,
        ).wait_recv()

    lax.fori_loop(0, last, add_step, 0)
    for d, c in streams:
        wait_add(d, c, last)
        out_ref[d, c, block(d, 1)] = summed(d, c, last)
        back_copy(d, c, 0).start()

    def back_step(step, carry):
        for d, c in streams:
            back_copy(d, c, step).wait_recv()
            back_copy(d, c, step + 1).start()
        return carry

    lax.fori_loop(0, last, back_step, 0)
    for d, c in streams:
        back_copy(d, c, last).wait_recv()

    def finish(step, carry):
        for d, c in streams:
            add_copy(d, c, step, True).wait_send()
            back_copy(d, c, step).wait_send()
        return carry

    lax.fori_loop(0, size - 1, finish, 0)


def sum_over_groups(terms):
    size = lax.axis_size("dp")
    rows, features = terms.shape
    unit = 2 * CUTS * size * 16
    padded = -(-rows // unit) * unit
    if padded != rows:
        terms = jnp.pad(terms, ((0, padded - rows), (0, 0)))
    piece = padded // (2 * CUTS * size)
    blocks = terms.reshape(2, CUTS, size, piece, features)
    slots = pltpu.VMEM((2, CUTS, size - 1, piece, features), BF16)
    signals = pltpu.SemaphoreType.DMA((2, CUTS, size - 1))
    out = pl.pallas_call(
        functools.partial(sum_kernel, size, CUTS),
        out_shape=jax.ShapeDtypeStruct(blocks.shape, BF16),
        in_specs=[pl.BlockSpec(memory_space=pltpu.VMEM)],
        out_specs=pl.BlockSpec(memory_space=pltpu.VMEM),
        scratch_shapes=[slots, slots, signals, signals, signals, signals],
        compiler_params=pltpu.CompilerParams(
            collective_id=0, has_side_effects=True, vmem_limit_bytes=40 * 1024 * 1024
        ),
    )(blocks)
    return out.reshape(padded, features)[:rows]


def shards(
    frames, dec_states, out_grad, frame_lengths, token_lengths, weights, norm_gains, norm_biases
):
    matrices = weights[0]
    head_cols, features = matrices.shape[1:]
    terms = section_terms(
        frames, dec_states, out_grad, frame_lengths, token_lengths, matrices, norm_gains,
        norm_biases,
    )
    gradient = sum_over_groups(terms.reshape(3 * head_cols, features)).astype(F32)
    return gradient.reshape(1, 3, head_cols, features)


def solution(mesh):
    placed = (
        P(None, ("dp", "mp"), None),
        P(None, "dp", None),
        P(None, "dp", None),
        P(None, "dp", None),
        P(None, "dp", None),
        P("segment", None, "mp", None),
        P(),
        P(),
    )
    return jax.shard_map(
        shards,
        mesh=mesh,
        in_specs=placed,
        out_specs=P("segment", None, "mp", None),
        check_vma=False,
    )
```

```python
import functools
import math

import jax
import jax.numpy as jnp
from jax import lax
from jax.experimental import pallas as pl
from jax.experimental.pallas import tpu as pltpu
from jax.sharding import PartitionSpec as P

HS = 64
EPSILON = 1e-05
MESH = pl.DeviceIdType.MESH
F32 = jnp.float32
BF16 = jnp.bfloat16
NEAR = 2
CUTS = 2


def dot_rows(left, right):
    return lax.dot_general(left, right, (((1,), (1,)), ((), ())), preferred_element_type=F32)


def dot_plain(left, right):
    return lax.dot_general(left, right, (((1,), (0,)), ((), ())), preferred_element_type=F32)


def dot_outer(left, right):
    return lax.dot_general(left, right, (((0,), (0,)), ((), ())), preferred_element_type=F32)


def standardize(values):
    center = values - jnp.mean(values, axis=-1, keepdims=True)
    inverse = lax.rsqrt(jnp.mean(center * center, axis=-1, keepdims=True) + EPSILON)
    return center * inverse, inverse


def flat(rows):
    return rows.reshape(rows.shape[0] * rows.shape[1], rows.shape[2])


def utterance_ids(lengths_ref, m, shape, dim):
    places = lax.broadcasted_iota(jnp.int32, shape, dim)
    ids = jnp.zeros(shape, jnp.int32)
    bound = jnp.int32(0)
    for utterance in range(lengths_ref.shape[1]):
        bound = bound + lengths_ref[m, utterance]
        ids = ids + jnp.where(places >= bound, 1, 0)
    return ids


def mask_bias(frame_lens, other_lens, m, frame_count, other_count):
    shape = (frame_count, other_count)
    same = utterance_ids(frame_lens, m, shape, 0) == utterance_ids(other_lens, m, shape, 1)
    return jnp.where(same, 0.0, -1e30).astype(F32)


def head_probs(key_rows, queries, bias):
    scores = dot_rows(key_rows, queries) + bias
    raised = jnp.exp(scores - jnp.max(scores, axis=0, keepdims=True))
    return raised * (1.0 / jnp.sum(raised, axis=0, keepdims=True))


def head_scores_grad(probs, value_rows, grad_rows):
    grad_probs = dot_rows(value_rows, grad_rows)
    return (probs * (grad_probs - jnp.sum(grad_probs * probs, axis=0, keepdims=True))).astype(BF16)


def section_kernel(
    parts, frame_lens, token_lens, frames, tokens_in, upstream_in, weights_in, gains, biases,
    terms, tokens, upstream, weights, local_sem, full, normed, queries, key_rows, value_rows, context, probs, part, inbox, states, state_grad,
    key_grad, value_grad, bias, dec_bias, dec_queries, dec_grad, dec_context,
    frame_send, frame_recv, pass_send, pass_recv, part_send, part_recv, state_send, state_recv,
):
    section = lax.axis_index("segment")
    place = lax.axis_index("mp")
    micro_count, shard_rows, features = frames.shape
    frame_count = shard_rows * parts
    token_count = tokens.shape[1]
    head_cols = weights.shape[1]
    heads = head_cols // HS
    scaling = 1.0 / math.sqrt(HS)

    moves = [(frames.at[m], full.at[m, place]) for m in range(micro_count)]
    moves += [(tokens_in, tokens), (upstream_in, upstream)]
    moves += [(weights_in.at[i], weights.at[i]) for i in range(weights.shape[0])]
    loads = [
        pltpu.make_async_copy(source, target, local_sem.at[i])
        for i, (source, target) in enumerate(moves)
    ]
    for load in loads:
        load.start()

    barrier = pltpu.get_barrier_semaphore()
    for apart in range(parts):
        for side in range(2):
            if apart == 0 and side == 0:
                continue
            pl.semaphore_signal(
                barrier,
                inc=1,
                device_id={
                    "segment": lax.rem(section + side, 2),
                    "mp": lax.rem(place + apart, parts),
                },
                device_id_type=MESH,
            )
    pl.semaphore_wait(barrier, 2 * parts - 1)

    def copy_to(source, target, sends, recvs, side, apart):
        return pltpu.make_async_remote_copy(
            src_ref=source,
            dst_ref=target,
            send_sem=sends,
            recv_sem=recvs,
            device_id={"segment": side, "mp": lax.rem(place + apart, parts)},
            device_id_type=MESH,
        )

    def frame_copy(m, apart):
        return copy_to(
            frames.at[m], full.at[m, place], frame_send.at[m, apart], frame_recv.at[m, apart],
            0, apart,
        )

    def pass_copy(m, apart):
        origin = lax.rem(place - apart + parts, parts)
        return copy_to(
            full.at[m, origin], full.at[m, origin], pass_send.at[m, apart],
            pass_recv.at[m, apart], 1, 0,
        )

    def part_copy(m, apart, side):
        return copy_to(
            part.at[m], inbox.at[m, apart], part_send.at[m, apart], part_recv.at[m, apart],
            side, apart,
        )

    def state_copy(m):
        return copy_to(states.at[m], states.at[m], state_send.at[m], state_recv.at[m], 0, 0)

    def send_parts(m, side):
        for apart in range(1, parts):
            part_copy(m, apart, side).start()
        part_copy(m, 0, side).start()

    def received_sum(m, side):
        total = None
        for apart in range(parts):
            part_copy(m, apart, side).wait_recv()
            piece = inbox[m, apart].astype(F32)
            total = piece if total is None else total + piece
        return total

    def store_terms(last_left, last_right):
        block = min(256, head_cols)
        sources = ((key_grad, normed), (value_grad, normed), (last_left, last_right))
        for index, (left, right) in enumerate(sources):
            wide = flat(right[...])
            for start in range(0, head_cols, block):
                columns = slice(start, start + block)
                terms[index, columns, :] = dot_outer(flat(left[:, :, columns]), wide).astype(BF16)

    def encoder_forward(m, carry):
        for apart in range(1, parts):
            frame_copy(m, apart).wait_recv()
        for apart in range(1, parts):
            pass_copy(m, apart).start()
        rows, _ = standardize(flat(full[m]).astype(F32))
        normed[m] = (rows * gains[0:1, :] + biases[0:1, :]).astype(BF16)
        row_input = normed[m]
        queries[m] = (dot_rows(row_input, weights[0]).astype(BF16) * scaling).astype(BF16)
        key_rows[m] = dot_rows(row_input, weights[1]).astype(BF16)
        value_rows[m] = dot_rows(row_input, weights[2]).astype(BF16)
        bias[...] = mask_bias(frame_lens, frame_lens, m, frame_count, frame_count)
        for h in range(heads):
            cols = slice(h * HS, (h + 1) * HS)
            head = head_probs(key_rows[m, :, cols], queries[m, :, cols], bias[...]).astype(BF16)
            probs[m, h] = head
            context[m, :, cols] = dot_outer(head, value_rows[m, :, cols]).astype(BF16)
        part[m] = dot_plain(context[m], weights[3]).astype(BF16)
        send_parts(m, 1)
        return carry

    def encoder_backward(m, carry):
        grad_out = received_sum(m, 0)
        state_copy(m).wait_recv()
        rows, inverse = standardize(states[m].astype(F32))
        scaled = grad_out * gains[2:3, :]
        state_grad[m] = (
            inverse
            * (
                scaled
                - jnp.mean(scaled, axis=-1, keepdims=True)
                - rows * jnp.mean(scaled * rows, axis=-1, keepdims=True)
            )
        ).astype(BF16)
        grad_rows = dot_rows(state_grad[m], weights[3]).astype(BF16)
        key_rows[m] = grad_rows
        for h in range(heads):
            cols = slice(h * HS, (h + 1) * HS)
            grad_head = key_rows[m, :, cols]
            head = probs[m, h]
            change = head_scores_grad(head.astype(F32), value_rows[m, :, cols], grad_head)
            key_grad[m, :, cols] = dot_plain(change, queries[m, :, cols]).astype(BF16)
            value_grad[m, :, cols] = dot_plain(head, grad_head).astype(BF16)
        return carry

    def decoder_step(m, carry):
        for apart in range(1, parts):
            pass_copy(m, apart).wait_recv()
        total = received_sum(m, 1)
        states[m] = (flat(full[m]).astype(F32) + total).astype(BF16)
        state_copy(m).start()
        rows, _ = standardize(states[m].astype(F32))
        normed[m] = (rows * gains[2:3, :] + biases[2:3, :]).astype(BF16)
        row_input = normed[m]
        key_rows[m] = dot_rows(row_input, weights[1]).astype(BF16)
        value_rows[m] = dot_rows(row_input, weights[2]).astype(BF16)
        dec_bias[...] = mask_bias(frame_lens, token_lens, m, frame_count, token_count)
        for h in range(heads):
            cols = slice(h * HS, (h + 1) * HS)
            query_head = dec_queries[m, :, cols]
            value_head = value_rows[m, :, cols]
            grad_head = dec_grad[m, :, cols]
            exact = head_probs(key_rows[m, :, cols], query_head, dec_bias[...])
            head = exact.astype(BF16)
            dec_context[m, :, cols] = dot_outer(head, value_head).astype(BF16)
            change = head_scores_grad(exact, value_head, grad_head)
            key_grad[m, :, cols] = dot_plain(change, query_head).astype(BF16)
            value_grad[m, :, cols] = dot_plain(head, grad_head).astype(BF16)
        part[m] = (
            dot_plain(key_grad[m], weights[1]) + dot_plain(value_grad[m], weights[2])
        ).astype(BF16)
        send_parts(m, 0)
        return carry

    @pl.when(section == 0)
    def _():
        for m in range(micro_count):
            for apart in range(1, parts):
                frame_copy(m, apart).start()
        for load in loads:
            load.wait()
        lax.fori_loop(0, micro_count, encoder_forward, 0)
        lax.fori_loop(0, micro_count, encoder_backward, 0)
        store_terms(context, state_grad)
        for m in range(micro_count):
            for apart in range(1, parts):
                frame_copy(m, apart).wait_send()
                pass_copy(m, apart).wait_send()
            for apart in range(parts):
                part_copy(m, apart, 1).wait_send()

    @pl.when(section == 1)
    def _():
        for load in loads:
            load.wait()
        rows, _ = standardize(flat(tokens[...]).astype(F32))
        token_rows = (rows * gains[1:2, :] + biases[1:2, :]).astype(BF16)
        small = (micro_count, token_count, head_cols)
        token_queries = dot_rows(token_rows, weights[0]).astype(BF16) * scaling
        dec_queries[...] = token_queries.astype(BF16).reshape(small)
        dec_grad[...] = dot_rows(flat(upstream[...]), weights[3]).astype(BF16).reshape(small)
        lax.fori_loop(0, micro_count, decoder_step, 0)
        store_terms(dec_context, upstream)
        for m in range(micro_count):
            state_copy(m).wait_send()
            for apart in range(parts):
                part_copy(m, apart, 0).wait_send()


def section_terms(
    frames, dec_states, out_grad, frame_lengths, token_lengths, matrices, norm_gains, norm_biases
):
    parts = lax.axis_size("mp")
    micro_count, shard_rows, features = frames.shape
    frame_count = shard_rows * parts
    token_count = dec_states.shape[1]
    head_cols = matrices.shape[1]
    dma = pltpu.SemaphoreType.DMA
    wide = pltpu.VMEM((micro_count, frame_count, features), BF16)
    thin = pltpu.VMEM((micro_count, frame_count, head_cols), BF16)
    small = pltpu.VMEM((micro_count, token_count, head_cols), BF16)
    pairs = dma((micro_count, parts))
    return pl.pallas_call(
        functools.partial(section_kernel, parts),
        out_shape=jax.ShapeDtypeStruct((3, head_cols, features), BF16),
        in_specs=[pl.BlockSpec(memory_space=pltpu.SMEM)] * 2
        + [pl.BlockSpec(memory_space=pl.ANY)] * 4
        + [pl.BlockSpec(memory_space=pltpu.VMEM)] * 2,
        out_specs=pl.BlockSpec(memory_space=pltpu.VMEM),
        scratch_shapes=[
            pltpu.VMEM(dec_states.shape, BF16),
            pltpu.VMEM(out_grad.shape, BF16),
            pltpu.VMEM(matrices.shape, BF16),
            dma((micro_count + 2 + matrices.shape[0],)),
            pltpu.VMEM((micro_count, parts, shard_rows, features), BF16),
            wide,
            thin,
            thin,
            thin,
            thin,
            pltpu.VMEM((micro_count, head_cols // HS, frame_count, frame_count), BF16),
            wide,
            pltpu.VMEM((micro_count, parts, frame_count, features), BF16),
            wide,
            wide,
            thin,
            thin,
            pltpu.VMEM((frame_count, frame_count), F32),
            pltpu.VMEM((frame_count, token_count), F32),
            small,
            small,
            small,
            pairs,
            pairs,
            pairs,
            pairs,
            pairs,
            pairs,
            dma((micro_count,)),
            dma((micro_count,)),
        ],
        compiler_params=pltpu.CompilerParams(
            collective_id=1, has_side_effects=True, vmem_limit_bytes=60 * 1024 * 1024
        ),
    )(
        frame_lengths[:, 0], token_lengths[:, 0], frames, dec_states, out_grad, matrices,
        norm_gains, norm_biases,
    )


def sum_kernel(
    size, cuts, terms_ref, out_ref, g_ref, load_sem, held, inbox, add_send, add_recv, back_send, back_recv
):
    near = NEAR
    far = size // near
    me = lax.axis_index("dp")
    b = lax.rem(me, near)
    a = lax.div(me, near)
    place = jnp.where(b == 0, a, 2 * far - 1 - a)

    def device_at(spot):
        spot = lax.rem(spot + size, size)
        return jnp.where(spot < far, spot * near, (2 * far - 1 - spot) * near + 1)

    ways = (1, -1)
    peers = [device_at(place + way) for way in ways]
    load = pltpu.make_async_copy(terms_ref, g_ref, load_sem)
    load.start()

    barrier = pltpu.get_barrier_semaphore()
    for peer in peers:
        pl.semaphore_signal(barrier, inc=1, device_id={"dp": peer}, device_id_type=MESH)
    pl.semaphore_wait(barrier, 2)

    def block(d, apart):
        return lax.rem(place + ways[d] * apart + 2 * size, size)

    def add_copy(d, c, step, first):
        source = terms_ref.at[d, c, block(d, 0)] if first else held.at[d, c, step - 1]
        return pltpu.make_async_remote_copy(
            src_ref=source,
            dst_ref=inbox.at[d, c, step],
            send_sem=add_send.at[d, c, step],
            recv_sem=add_recv.at[d, c, step],
            device_id={"dp": peers[d]},
            device_id_type=MESH,
        )

    def back_copy(d, c, step):
        ref = out_ref.at[d, c, block(d, 1 - step)]
        return pltpu.make_async_remote_copy(
            src_ref=ref,
            dst_ref=ref,
            send_sem=back_send.at[d, c, step],
            recv_sem=back_recv.at[d, c, step],
            device_id={"dp": peers[d]},
            device_id_type=MESH,
        )

    streams = [(d, c) for c in range(cuts) for d in range(2)]
    last = size - 2

    def summed(d, c, step):
        mine = g_ref[d, c, block(d, -step - 1)].astype(F32)
        return (mine + inbox[d, c, step].astype(F32)).astype(BF16)

    for d, c in streams:
        add_copy(d, c, 0, True).start()
    load.wait()

    def add_step(step, carry):
        for d, c in streams:
            wait_add(d, c, step)
            held[d, c, step] = summed(d, c, step)
            add_copy(d, c, step + 1, False).start()
        return carry

    def wait_add(d, c, step):
        pltpu.make_async_remote_copy(
            src_ref=held.at[d, c, step],
            dst_ref=inbox.at[d, c, step],
            send_sem=add_send.at[d, c, step],
            recv_sem=add_recv.at[d, c, step],
            device_id={"dp": peers[d]},
            device_id_type=MESH,
        ).wait_recv()

    lax.fori_loop(0, last, add_step, 0)
    for d, c in streams:
        wait_add(d, c, last)
        out_ref[d, c, block(d, 1)] = summed(d, c, last)
        back_copy(d, c, 0).start()

    def back_step(step, carry):
        for d, c in streams:
            back_copy(d, c, step).wait_recv()
            back_copy(d, c, step + 1).start()
        return carry

    lax.fori_loop(0, last, back_step, 0)
    for d, c in streams:
        back_copy(d, c, last).wait_recv()

    def finish(step, carry):
        for d, c in streams:
            add_copy(d, c, step, True).wait_send()
            back_copy(d, c, step).wait_send()
        return carry

    lax.fori_loop(0, size - 1, finish, 0)


def sum_over_groups(terms):
    size = lax.axis_size("dp")
    rows, features = terms.shape
    unit = 2 * CUTS * size * 16
    padded = -(-rows // unit) * unit
    if padded != rows:
        terms = jnp.pad(terms, ((0, padded - rows), (0, 0)))
    piece = padded // (2 * CUTS * size)
    blocks = terms.reshape(2, CUTS, size, piece, features)
    slots = pltpu.VMEM((2, CUTS, size - 1, piece, features), BF16)
    signals = pltpu.SemaphoreType.DMA((2, CUTS, size - 1))
    out = pl.pallas_call(
        functools.partial(sum_kernel, size, CUTS),
        out_shape=jax.ShapeDtypeStruct(blocks.shape, BF16),
        in_specs=[pl.BlockSpec(memory_space=pl.ANY)],
        out_specs=pl.BlockSpec(memory_space=pltpu.VMEM),
        scratch_shapes=[
            pltpu.VMEM(blocks.shape, BF16), pltpu.SemaphoreType.DMA, slots, slots, signals, signals, signals, signals,
        ],
        compiler_params=pltpu.CompilerParams(
            collective_id=0, has_side_effects=True, vmem_limit_bytes=60 * 1024 * 1024
        ),
    )(blocks)
    return out.reshape(padded, features)[:rows]


def shards(
    frames, dec_states, out_grad, frame_lengths, token_lengths, weights, norm_gains, norm_biases
):
    matrices = weights[0]
    head_cols, features = matrices.shape[1:]
    terms = section_terms(
        frames, dec_states, out_grad, frame_lengths, token_lengths, matrices, norm_gains,
        norm_biases,
    )
    gradient = sum_over_groups(terms.reshape(3 * head_cols, features)).astype(F32)
    return gradient.reshape(1, 3, head_cols, features)


def solution(mesh):
    placed = (
        P(None, ("dp", "mp"), None),
        P(None, "dp", None),
        P(None, "dp", None),
        P(None, "dp", None),
        P(None, "dp", None),
        P("segment", None, "mp", None),
        P(),
        P(),
    )
    return jax.shard_map(
        shards,
        mesh=mesh,
        in_specs=placed,
        out_specs=P("segment", None, "mp", None),
        check_vma=False,
    )
```

```python
import functools
import math

import jax
import jax.numpy as jnp
from jax import lax
from jax.experimental import pallas as pl
from jax.experimental.pallas import tpu as pltpu
from jax.sharding import PartitionSpec as P

HS = 64
EPSILON = 1e-05
MESH = pl.DeviceIdType.MESH
F32 = jnp.float32
BF16 = jnp.bfloat16
NEAR = 2
CUTS = 2


def dot_rows(left, right):
    return lax.dot_general(left, right, (((1,), (1,)), ((), ())), preferred_element_type=F32)


def dot_plain(left, right):
    return lax.dot_general(left, right, (((1,), (0,)), ((), ())), preferred_element_type=F32)


def dot_outer(left, right):
    return lax.dot_general(left, right, (((0,), (0,)), ((), ())), preferred_element_type=F32)


def standardize(values):
    center = values - jnp.mean(values, axis=-1, keepdims=True)
    inverse = lax.rsqrt(jnp.mean(center * center, axis=-1, keepdims=True) + EPSILON)
    return center * inverse, inverse


def flat(rows):
    return rows.reshape(rows.shape[0] * rows.shape[1], rows.shape[2])


def utterance_ids(lengths_ref, m, shape, dim):
    places = lax.broadcasted_iota(jnp.int32, shape, dim)
    ids = jnp.zeros(shape, jnp.int32)
    bound = jnp.int32(0)
    for utterance in range(lengths_ref.shape[1]):
        bound = bound + lengths_ref[m, utterance]
        ids = ids + jnp.where(places >= bound, 1, 0)
    return ids


def mask_bias(frame_lens, other_lens, m, frame_count, other_count):
    shape = (frame_count, other_count)
    same = utterance_ids(frame_lens, m, shape, 0) == utterance_ids(other_lens, m, shape, 1)
    return jnp.where(same, 0.0, -1e30).astype(F32)


def head_probs(key_rows, queries, bias):
    scores = dot_rows(key_rows, queries) + bias
    raised = jnp.exp(scores - jnp.max(scores, axis=0, keepdims=True))
    return raised * (1.0 / jnp.sum(raised, axis=0, keepdims=True))


def head_scores_grad(probs, value_rows, grad_rows):
    grad_probs = dot_rows(value_rows, grad_rows)
    return (probs * (grad_probs - jnp.sum(grad_probs * probs, axis=0, keepdims=True))).astype(BF16)


def section_kernel(
    parts, frame_lens, token_lens, frames, tokens_in, upstream_in, weights_in, gains, biases,
    terms, tokens, upstream, weights, local_sem, full, normed, queries, key_rows, value_rows, context, probs, part, inbox, states, state_grad,
    key_grad, value_grad, bias, dec_bias, dec_queries, dec_grad, dec_context,
    frame_send, frame_recv, pass_send, pass_recv, part_send, part_recv, state_send, state_recv,
):
    section = lax.axis_index("segment")
    place = lax.axis_index("mp")
    micro_count, shard_rows, features = frames.shape
    frame_count = shard_rows * parts
    token_count = tokens.shape[1]
    head_cols = weights.shape[1]
    heads = head_cols // HS
    scaling = 1.0 / math.sqrt(HS)

    moves = [(frames.at[m], full.at[m, place]) for m in range(micro_count)]
    moves += [(tokens_in, tokens), (upstream_in, upstream)]
    moves += [(weights_in.at[i], weights.at[i]) for i in range(weights.shape[0])]
    loads = [
        pltpu.make_async_copy(source, target, local_sem.at[i])
        for i, (source, target) in enumerate(moves)
    ]
    for load in loads:
        load.start()

    barrier = pltpu.get_barrier_semaphore()
    for apart in range(parts):
        for side in range(2):
            if apart == 0 and side == 0:
                continue
            pl.semaphore_signal(
                barrier,
                inc=1,
                device_id={
                    "segment": lax.rem(section + side, 2),
                    "mp": lax.rem(place + apart, parts),
                },
                device_id_type=MESH,
            )
    pl.semaphore_wait(barrier, 2 * parts - 1)

    def copy_to(source, target, sends, recvs, side, apart):
        return pltpu.make_async_remote_copy(
            src_ref=source,
            dst_ref=target,
            send_sem=sends,
            recv_sem=recvs,
            device_id={"segment": side, "mp": lax.rem(place + apart, parts)},
            device_id_type=MESH,
        )

    def frame_copy(m, apart):
        return copy_to(
            frames.at[m], full.at[m, place], frame_send.at[m, apart], frame_recv.at[m, apart],
            0, apart,
        )

    def pass_copy(m, apart):
        origin = lax.rem(place - apart + parts, parts)
        return copy_to(
            full.at[m, origin], full.at[m, origin], pass_send.at[m, apart],
            pass_recv.at[m, apart], 1, 0,
        )

    def part_copy(m, apart, side):
        return copy_to(
            part.at[m], inbox.at[m, apart], part_send.at[m, apart], part_recv.at[m, apart],
            side, apart,
        )

    def state_copy(m):
        return copy_to(states.at[m], states.at[m], state_send.at[m], state_recv.at[m], 0, 0)

    def send_parts(m, side):
        for apart in range(1, parts):
            part_copy(m, apart, side).start()
        part_copy(m, 0, side).start()

    def received_sum(m, side):
        total = None
        for apart in range(parts):
            part_copy(m, apart, side).wait_recv()
            piece = inbox[m, apart].astype(F32)
            total = piece if total is None else total + piece
        return total

    def store_terms(last_left, last_right):
        block = min(256, head_cols)
        sources = ((key_grad, normed), (value_grad, normed), (last_left, last_right))
        for index, (left, right) in enumerate(sources):
            wide = flat(right[...])
            for start in range(0, head_cols, block):
                columns = slice(start, start + block)
                terms[index, columns, :] = dot_outer(flat(left[:, :, columns]), wide).astype(BF16)

    def encoder_forward(m, carry):
        for apart in range(1, parts):
            frame_copy(m, apart).wait_recv()
        for apart in range(1, parts):
            pass_copy(m, apart).start()
        rows, _ = standardize(flat(full[m]).astype(F32))
        normed[m] = (rows * gains[0:1, :] + biases[0:1, :]).astype(BF16)
        row_input = normed[m]
        queries[m] = (dot_rows(row_input, weights[0]).astype(BF16) * scaling).astype(BF16)
        key_rows[m] = dot_rows(row_input, weights[1]).astype(BF16)
        value_rows[m] = dot_rows(row_input, weights[2]).astype(BF16)
        bias[...] = mask_bias(frame_lens, frame_lens, m, frame_count, frame_count)
        for h in range(heads):
            cols = slice(h * HS, (h + 1) * HS)
            head = head_probs(key_rows[m, :, cols], queries[m, :, cols], bias[...]).astype(BF16)
            probs[m, h] = head
            context[m, :, cols] = dot_outer(head, value_rows[m, :, cols]).astype(BF16)
        part[m] = dot_plain(context[m], weights[3]).astype(BF16)
        send_parts(m, 1)
        return carry

    def encoder_backward(m, carry):
        grad_out = received_sum(m, 0)
        state_copy(m).wait_recv()
        rows, inverse = standardize(states[m].astype(F32))
        scaled = grad_out * gains[2:3, :]
        state_grad[m] = (
            inverse
            * (
                scaled
                - jnp.mean(scaled, axis=-1, keepdims=True)
                - rows * jnp.mean(scaled * rows, axis=-1, keepdims=True)
            )
        ).astype(BF16)
        grad_rows = dot_rows(state_grad[m], weights[3]).astype(BF16)
        key_rows[m] = grad_rows
        for h in range(heads):
            cols = slice(h * HS, (h + 1) * HS)
            grad_head = key_rows[m, :, cols]
            head = probs[m, h]
            change = head_scores_grad(head.astype(F32), value_rows[m, :, cols], grad_head)
            key_grad[m, :, cols] = dot_plain(change, queries[m, :, cols]).astype(BF16)
            value_grad[m, :, cols] = dot_plain(head, grad_head).astype(BF16)
        return carry

    def decoder_step(m, carry):
        for apart in range(1, parts):
            pass_copy(m, apart).wait_recv()
        total = received_sum(m, 1)
        states[m] = (flat(full[m]).astype(F32) + total).astype(BF16)
        state_copy(m).start()
        rows, _ = standardize(states[m].astype(F32))
        normed[m] = (rows * gains[2:3, :] + biases[2:3, :]).astype(BF16)
        row_input = normed[m]
        key_rows[m] = dot_rows(row_input, weights[1]).astype(BF16)
        value_rows[m] = dot_rows(row_input, weights[2]).astype(BF16)
        dec_bias[...] = mask_bias(frame_lens, token_lens, m, frame_count, token_count)
        for h in range(heads):
            cols = slice(h * HS, (h + 1) * HS)
            query_head = dec_queries[m, :, cols]
            value_head = value_rows[m, :, cols]
            grad_head = dec_grad[m, :, cols]
            exact = head_probs(key_rows[m, :, cols], query_head, dec_bias[...])
            head = exact.astype(BF16)
            dec_context[m, :, cols] = dot_outer(head, value_head).astype(BF16)
            change = head_scores_grad(exact, value_head, grad_head)
            key_grad[m, :, cols] = dot_plain(change, query_head).astype(BF16)
            value_grad[m, :, cols] = dot_plain(head, grad_head).astype(BF16)
        part[m] = (
            dot_plain(key_grad[m], weights[1]) + dot_plain(value_grad[m], weights[2])
        ).astype(BF16)
        send_parts(m, 0)
        return carry

    @pl.when(section == 0)
    def _():
        for m in range(micro_count):
            for apart in range(1, parts):
                frame_copy(m, apart).start()
        for load in loads:
            load.wait()
        lax.fori_loop(0, micro_count, encoder_forward, 0)
        lax.fori_loop(0, micro_count, encoder_backward, 0)
        store_terms(context, state_grad)
        for m in range(micro_count):
            for apart in range(1, parts):
                frame_copy(m, apart).wait_send()
                pass_copy(m, apart).wait_send()
            for apart in range(parts):
                part_copy(m, apart, 1).wait_send()

    @pl.when(section == 1)
    def _():
        for load in loads:
            load.wait()
        rows, _ = standardize(flat(tokens[...]).astype(F32))
        token_rows = (rows * gains[1:2, :] + biases[1:2, :]).astype(BF16)
        small = (micro_count, token_count, head_cols)
        token_queries = dot_rows(token_rows, weights[0]).astype(BF16) * scaling
        dec_queries[...] = token_queries.astype(BF16).reshape(small)
        dec_grad[...] = dot_rows(flat(upstream[...]), weights[3]).astype(BF16).reshape(small)
        lax.fori_loop(0, micro_count, decoder_step, 0)
        store_terms(dec_context, upstream)
        for m in range(micro_count):
            state_copy(m).wait_send()
            for apart in range(parts):
                part_copy(m, apart, 0).wait_send()


def section_terms(
    frames, dec_states, out_grad, frame_lengths, token_lengths, matrices, norm_gains, norm_biases
):
    parts = lax.axis_size("mp")
    micro_count, shard_rows, features = frames.shape
    frame_count = shard_rows * parts
    token_count = dec_states.shape[1]
    head_cols = matrices.shape[1]
    dma = pltpu.SemaphoreType.DMA
    wide = pltpu.VMEM((micro_count, frame_count, features), BF16)
    thin = pltpu.VMEM((micro_count, frame_count, head_cols), BF16)
    small = pltpu.VMEM((micro_count, token_count, head_cols), BF16)
    pairs = dma((micro_count, parts))
    return pl.pallas_call(
        functools.partial(section_kernel, parts),
        out_shape=jax.ShapeDtypeStruct((3, head_cols, features), BF16),
        in_specs=[pl.BlockSpec(memory_space=pltpu.SMEM)] * 2
        + [pl.BlockSpec(memory_space=pl.ANY)] * 4
        + [pl.BlockSpec(memory_space=pltpu.VMEM)] * 2,
        out_specs=pl.BlockSpec(memory_space=pltpu.VMEM),
        scratch_shapes=[
            pltpu.VMEM(dec_states.shape, BF16),
            pltpu.VMEM(out_grad.shape, BF16),
            pltpu.VMEM(matrices.shape, BF16),
            dma((micro_count + 2 + matrices.shape[0],)),
            pltpu.VMEM((micro_count, parts, shard_rows, features), BF16),
            wide,
            thin,
            thin,
            thin,
            thin,
            pltpu.VMEM((micro_count, head_cols // HS, frame_count, frame_count), BF16),
            wide,
            pltpu.VMEM((micro_count, parts, frame_count, features), BF16),
            wide,
            wide,
            thin,
            thin,
            pltpu.VMEM((frame_count, frame_count), F32),
            pltpu.VMEM((frame_count, token_count), F32),
            small,
            small,
            small,
            pairs,
            pairs,
            pairs,
            pairs,
            pairs,
            pairs,
            dma((micro_count,)),
            dma((micro_count,)),
        ],
        compiler_params=pltpu.CompilerParams(
            collective_id=1, has_side_effects=True, vmem_limit_bytes=60 * 1024 * 1024
        ),
    )(
        frame_lengths[:, 0], token_lengths[:, 0], frames, dec_states, out_grad, matrices,
        norm_gains, norm_biases,
    )


def sum_kernel(
    size, cuts, g_ref, out_ref, held, inbox, add_send, add_recv, back_send, back_recv
):
    near = NEAR
    far = size // near
    me = lax.axis_index("dp")
    b = lax.rem(me, near)
    a = lax.div(me, near)
    place = jnp.where(b == 0, a, 2 * far - 1 - a)

    def device_at(spot):
        spot = lax.rem(spot + size, size)
        return jnp.where(spot < far, spot * near, (2 * far - 1 - spot) * near + 1)

    ways = (1, -1)
    peers = [device_at(place + way) for way in ways]

    barrier = pltpu.get_barrier_semaphore()
    for peer in peers:
        pl.semaphore_signal(barrier, inc=1, device_id={"dp": peer}, device_id_type=MESH)
    pl.semaphore_wait(barrier, 2)

    def block(d, apart):
        return lax.rem(place + ways[d] * apart + 2 * size, size)

    def add_copy(d, c, step, first):
        source = g_ref.at[d, c, block(d, 0)] if first else held.at[d, c, step - 1]
        return pltpu.make_async_remote_copy(
            src_ref=source,
            dst_ref=inbox.at[d, c, step],
            send_sem=add_send.at[d, c, step],
            recv_sem=add_recv.at[d, c, step],
            device_id={"dp": peers[d]},
            device_id_type=MESH,
        )

    def back_copy(d, c, step):
        ref = out_ref.at[d, c, block(d, 1 - step)]
        return pltpu.make_async_remote_copy(
            src_ref=ref,
            dst_ref=ref,
            send_sem=back_send.at[d, c, step],
            recv_sem=back_recv.at[d, c, step],
            device_id={"dp": peers[d]},
            device_id_type=MESH,
        )

    streams = [(d, c) for c in range(cuts) for d in range(2)]
    last = size - 2

    def summed(d, c, step):
        mine = g_ref[d, c, block(d, -step - 1)].astype(F32)
        return (mine + inbox[d, c, step].astype(F32)).astype(BF16)

    for d, c in streams:
        add_copy(d, c, 0, True).start()

    def add_step(step, carry):
        for d, c in streams:
            wait_add(d, c, step)
            held[d, c, step] = summed(d, c, step)
            add_copy(d, c, step + 1, False).start()
        return carry

    def wait_add(d, c, step):
        pltpu.make_async_remote_copy(
            src_ref=held.at[d, c, step],
            dst_ref=inbox.at[d, c, step],
            send_sem=add_send.at[d, c, step],
            recv_sem=add_recv.at[d, c, step],
            device_id={"dp": peers[d]},
            device_id_type=MESH,
        ).wait_recv()

    lax.fori_loop(0, last, add_step, 0)
    for d, c in streams:
        wait_add(d, c, last)
        out_ref[d, c, block(d, 1)] = summed(d, c, last)
        back_copy(d, c, 0).start()

    def back_step(step, carry):
        for d, c in streams:
            back_copy(d, c, step).wait_recv()
            back_copy(d, c, step + 1).start()
        return carry

    lax.fori_loop(0, last, back_step, 0)
    for d, c in streams:
        back_copy(d, c, last).wait_recv()

    def finish(step, carry):
        for d, c in streams:
            add_copy(d, c, step, True).wait_send()
            back_copy(d, c, step).wait_send()
        return carry

    lax.fori_loop(0, size - 1, finish, 0)


def sum_over_groups(terms):
    size = lax.axis_size("dp")
    rows, features = terms.shape
    unit = 2 * CUTS * size * 16
    padded = -(-rows // unit) * unit
    if padded != rows:
        terms = jnp.pad(terms, ((0, padded - rows), (0, 0)))
    piece = padded // (2 * CUTS * size)
    blocks = terms.reshape(2, CUTS, size, piece, features)
    slots = pltpu.VMEM((2, CUTS, size - 1, piece, features), BF16)
    signals = pltpu.SemaphoreType.DMA((2, CUTS, size - 1))
    out = pl.pallas_call(
        functools.partial(sum_kernel, size, CUTS),
        out_shape=jax.ShapeDtypeStruct(blocks.shape, BF16),
        in_specs=[pl.BlockSpec(memory_space=pltpu.VMEM)],
        out_specs=pl.BlockSpec(memory_space=pltpu.VMEM),
        scratch_shapes=[slots, slots, signals, signals, signals, signals],
        compiler_params=pltpu.CompilerParams(
            collective_id=0, has_side_effects=True, vmem_limit_bytes=40 * 1024 * 1024
        ),
    )(blocks)
    return out.reshape(padded, features)[:rows]


def shards(
    frames, dec_states, out_grad, frame_lengths, token_lengths, weights, norm_gains, norm_biases
):
    matrices = weights[0]
    head_cols, features = matrices.shape[1:]
    terms = section_terms(
        frames, dec_states, out_grad, frame_lengths, token_lengths, matrices, norm_gains,
        norm_biases,
    )
    gradient = sum_over_groups(terms.reshape(3 * head_cols, features)).astype(F32)
    return gradient.reshape(1, 3, head_cols, features)


def solution(mesh):
    placed = (
        P(None, ("dp", "mp"), None),
        P(None, "dp", None),
        P(None, "dp", None),
        P(None, "dp", None),
        P(None, "dp", None),
        P("segment", None, "mp", None),
        P(),
        P(),
    )
    return jax.shard_map(
        shards,
        mesh=mesh,
        in_specs=placed,
        out_specs=P("segment", None, "mp", None),
        check_vma=False,
    )
```
